32 devices in a mesh: exp: 8 (over y, x, core), seq: 4 (over z).
Axes of the slice: x: 2, y: 2, z: 4, core: 2. Of those that a mesh axis runs over, the one named last changes fastest.
Arguments:
- projected: bfloat16 [8, 512, 3, 16, 128], P('exp', 'seq'), may hold values from -5 to 5
- hidden_in: bfloat16 [8, 512, 2048], P('exp', 'seq'), may hold values from -6 to 6
- modulation: float32 [8, 4, 2048], P('exp'), may hold values from -4 to 4
- w_router: bfloat16 [2048, 8], replicated, may hold values from -0.125 to 0.125
- picked: int32 [8, 4, 8, 2], P('exp', 'seq'), may hold values from 0 to 511, as said below
- counts: int32 [8, 4, 8], P('exp', 'seq'), may hold values from 0 to 2, as said below
- weight_in: bfloat16 [8, 2048, 4096], P('exp', None, 'seq'), may hold values from -0.125 to 0.125
- weight_out: bfloat16 [8, 4096, 2048], P('exp', 'seq'), may hold values from -0.09375 to 0.09375
Outputs:
- layer_out: bfloat16 [8, 512, 2048], P('exp', 'seq')
The draws below stay inside these ranges and needn't reach their ends.
Inputs may be any that keep to these rules, and one draw needn't show every extreme that they name: picked[i, s, e, c] lies in shard s of image i, from s * 128 to s * 128 + 127; the entries of one block are distinct. `counts`: in every draw one expert has 2 live slots in every block, and every device's tokens fill all 2 slots of some expert.
All inputs are finite; a program needn't handle non-finite values.
Results may differ from the reference program's by a relative error of at most 0.007.
Values may be sent and summed in bfloat16 or wider, within the bound.
A program may use at most 64 MiB of HBM per device.

```python
import math
import jax
import jax.numpy as jnp
from jax import lax

D = 2048
HEADS = 16
HEAD = 128
FF = 4096
CAP = 2
TOK_DEV = 128
LENGTH = 512
IMAGES = 8
EXPERTS = 8
N_SEQ = 4


def draw_projected(key, part):
    key = jax.random.fold_in(key, 11)
    first_key = jax.random.fold_in(key, 0)
    shape = (IMAGES, LENGTH, 3, HEADS, HEAD)
    drawn = jnp.clip(1.4 * jax.random.normal(first_key, shape, jnp.float32), -5.0, 5.0)
    return drawn.astype(jnp.bfloat16)


def draw_picked(key, part):
    key = jax.random.fold_in(key, 5)
    first_key, second_key = jax.random.split(key)
    shards = LENGTH // TOK_DEV
    starting = jax.random.randint(first_key, (IMAGES, shards, EXPERTS, 1), 0, TOK_DEV, jnp.int32)
    stride = jax.random.randint(second_key, (IMAGES, shards, EXPERTS, 1), 1, TOK_DEV // CAP + 1, jnp.int32)
    slot_ids = lax.broadcasted_iota(jnp.int32, (IMAGES, shards, EXPERTS, CAP), 3)
    shard_ids = lax.broadcasted_iota(jnp.int32, (IMAGES, shards, EXPERTS, CAP), 1)
    local_positions = (starting + slot_ids * stride) % TOK_DEV
    return local_positions + shard_ids * TOK_DEV


def draw_counts(key, part):
    key = jax.random.fold_in(key, 7)
    first_key, second_key, third_key = jax.random.split(key, 3)
    shards = LENGTH // TOK_DEV
    shape = (IMAGES, shards, EXPERTS)
    live_counts = jax.random.randint(first_key, shape, 0, CAP + 1, jnp.int32)
    chosen = jax.random.randint(second_key, (IMAGES, shards, 1), 0, EXPERTS, jnp.int32)
    full_expert = jax.random.randint(third_key, (), 0, EXPERTS, jnp.int32)
    expert_ids = lax.broadcasted_iota(jnp.int32, shape, 2)
    filled = (expert_ids == chosen) | (expert_ids == full_expert)
    return jnp.where(filled, CAP, live_counts)


def block_levels(own_key, dims, cuts, low, top_value):
    factor_of = 1.0
    for dim, shards_of in cuts:
        draws = jax.random.uniform(jax.random.fold_in(jax.random.fold_in(own_key, 6), dim), (shards_of,), jnp.float32, low / len(cuts), top_value / len(cuts))
        factor_of = factor_of * jnp.repeat(jnp.exp(draws), dims[dim] // shards_of).reshape((-1,) + (1,) * (len(dims) - 1 - dim))
    return factor_of


def bell_draw(rng, shape, scale, bound, pieces=(), held_as=jnp.bfloat16):
    factor_of = block_levels(rng, shape, pieces, -0.22, 0.18) if pieces else 1.0
    values = jax.random.normal(rng, shape, jnp.float32) * scale * factor_of
    return jnp.minimum(jnp.maximum(values, -bound), bound).astype(held_as)


def setup_inputs(seed: int = 0) -> dict:
    seeds = jax.random.split(jax.random.key(seed), 9)
    return {
        "projected": draw_projected(jax.random.fold_in(seeds[8], 71), 0),
        "hidden_in": bell_draw(seeds[1], (IMAGES, LENGTH, D), 1.0, 6.0, ((0, 8), (1, 4))),
        "modulation": bell_draw(seeds[2], (IMAGES, 4, D), 1.0, 4.0, ((0, 8),), jnp.float32),
        "w_router": bell_draw(seeds[3], (D, EXPERTS), D ** -0.5, 0.125),
        "picked": draw_picked(jax.random.fold_in(seeds[8], 71), 0),
        "counts": draw_counts(jax.random.fold_in(seeds[8], 71), 0),
        "weight_in": bell_draw(seeds[6], (EXPERTS, D, FF), D ** -0.5, 0.125, ((0, 8), (2, 4))),
        "weight_out": bell_draw(seeds[7], (EXPERTS, FF, D), FF ** -0.5, 0.09375, ((0, 8), (1, 4))),
    }


epsilon_norm = 1e-06

def attend_head(queries, keys_all, values_all):
    length = queries.shape[0]
    block_size = min(512, length)
    score_scale = 1.0 / math.sqrt(queries.shape[1])

    def one_block(query_rows):
        scores = jnp.dot(query_rows, keys_all.T, preferred_element_type=jnp.float32) * score_scale
        top_score = lax.optimization_barrier(jnp.max(scores, axis=-1, keepdims=True))
        weights = jnp.exp(scores - top_score)
        weights = weights / lax.optimization_barrier(jnp.sum(weights, axis=-1, keepdims=True))
        return jnp.dot(weights.astype(jnp.bfloat16), values_all, preferred_element_type=jnp.float32).astype(jnp.bfloat16)
    blocked = queries.reshape(length // block_size, block_size, queries.shape[1])
    return lax.map(one_block, blocked).reshape(length, queries.shape[1])

def head_attention(head_data):
    return attend_head(head_data[:, 0], head_data[:, 1], head_data[:, 2])

def modulate(residual, shift_row, scale_row):
    average = lax.optimization_barrier(jnp.mean(residual, axis=-1, keepdims=True))
    centred = residual - average
    variance = lax.optimization_barrier(jnp.mean(centred * centred, axis=-1, keepdims=True))
    normed = centred * lax.rsqrt(variance + epsilon_norm)
    return (normed * (1.0 + scale_row) + shift_row).astype(jnp.bfloat16)

def reference(projected, hidden_in, modulation, w_router, picked, counts, weight_in, weight_out):
    per_head = jnp.moveaxis(projected, 3, 1).reshape(IMAGES * HEADS, LENGTH, 3, HEAD)
    attended = lax.map(head_attention, per_head)
    attended = jnp.moveaxis(attended.reshape(IMAGES, HEADS, LENGTH, HEAD), 1, 2).reshape(IMAGES, LENGTH, D)
    residual = hidden_in.astype(jnp.float32) + modulation[:, 0][:, None, :] * attended.astype(jnp.float32)
    modulated = modulate(residual, modulation[:, 1][:, None, :], modulation[:, 2][:, None, :])
    logits = jnp.dot(modulated.reshape(IMAGES * LENGTH, D), w_router, preferred_element_type=jnp.float32)
    gate_values = jax.nn.sigmoid(logits).reshape(IMAGES, LENGTH, EXPERTS)
    slot_live = jnp.arange(CAP, dtype=jnp.int32)[None, None, None, :] < counts[..., None]
    image_ids = jnp.arange(IMAGES, dtype=jnp.int32)[:, None, None]

    def add_expert(mixture, expert):
        positions = picked[:, :, expert, :]
        live_slots = slot_live[:, :, expert, :]
        row_data = jnp.where(live_slots[..., None], modulated[image_ids, positions], jnp.zeros((), modulated.dtype))
        hidden = jax.nn.gelu(jnp.dot(row_data.reshape(-1, D), weight_in[expert], preferred_element_type=jnp.float32), approximate=True).astype(jnp.bfloat16)
        blocks_in = hidden.reshape(-1, N_SEQ, FF // N_SEQ).astype(jnp.float32)
        blocks_out = weight_out[expert].reshape(N_SEQ, FF // N_SEQ, D).astype(jnp.float32)
        partial_value = jnp.einsum('rsf,sfd->srd', blocks_in, blocks_out, precision=lax.Precision.HIGHEST).astype(jnp.bfloat16)
        expert_rows = lax.optimization_barrier(jnp.sum(partial_value.astype(jnp.float32), axis=0)).astype(jnp.bfloat16).reshape(IMAGES, N_SEQ, CAP, D)
        slot_gate = gate_values[image_ids, positions, expert]
        slot_gate = jnp.where(live_slots, slot_gate, jnp.zeros((), slot_gate.dtype))
        mixture = mixture.at[image_ids, positions].add(slot_gate[..., None] * expert_rows.astype(jnp.float32))
        return (mixture, None)
    mixture, _ = lax.scan(add_expert, jnp.zeros((IMAGES, LENGTH, D), jnp.float32), jnp.arange(EXPERTS, dtype=jnp.int32))
    return (residual + modulation[:, 3][:, None, :] * mixture).astype(jnp.bfloat16)
```

```python
import functools
import math

import jax
import jax.numpy as jnp
from jax import lax
from jax.experimental import pallas as pl
from jax.experimental.pallas import tpu as pltpu
from jax.sharding import PartitionSpec as P

epsilon_norm = 1e-06
MESH = pl.DeviceIdType.MESH
BF = jnp.bfloat16
F32 = jnp.float32


def block_kernel(
    n_exp,
    n_seq,
    heads,
    cap,
    picked_ref,
    counts_ref,
    proj_hbm,
    hidden_hbm,
    mod_hbm,
    router_hbm,
    win_hbm,
    wout_hbm,
    out_ref,
    proj,
    hidden_in,
    mod,
    router,
    win,
    wout,
    wide,
    qkv_out,
    qkv_in,
    att_out,
    att_in,
    resid,
    stage,
    rows_out,
    rows_in,
    rows_x,
    ret_out,
    ret_in,
    rows_e,
    load_sem,
    qkv_send,
    qkv_recv,
    qkv_own,
    att_send,
    att_recv,
    att_own,
    row_send,
    row_recv,
    ret_send,
    ret_recv,
):
    me_e = lax.axis_index("exp")
    me_s = lax.axis_index("seq")
    devices = n_exp * n_seq
    toks = hidden_in.shape[0]
    width = hidden_in.shape[1]
    head = proj.shape[1]
    local_heads = heads // n_seq
    length = toks * n_seq
    slots = n_exp * cap
    pieces = width // head
    me = me_e * n_seq + me_s

    def peer_of(d):
        return (
            lax.rem(me_e + d // n_seq, n_exp),
            lax.rem(me_s + lax.rem(d, n_seq), n_seq),
        )

    barrier = pltpu.get_barrier_semaphore()

    def greet(d, carry):
        pl.semaphore_signal(barrier, inc=1, device_id=peer_of(d), device_id_type=MESH)
        return carry

    lax.fori_loop(1, devices, greet, 0)

    loads = [
        pltpu.make_async_copy(src, dst, load_sem.at[i])
        for i, (src, dst) in enumerate(
            (
                (proj_hbm, proj),
                (hidden_hbm, hidden_in),
                (mod_hbm, mod),
                (router_hbm, router),
                (win_hbm, win),
                (wout_hbm, wout),
            )
        )
    ]
    for load in loads:
        load.start()

    loads[0].wait()
    wide[...] = proj[...].astype(F32)
    qkv_copies = []
    for j in range(local_heads):
        for s in range(n_seq):
            for c in range(3):
                first = c * heads + s * local_heads + j
                qkv_out[j, s, c] = wide[pl.ds(first, toks, stride=3 * heads), :].astype(BF)
        if j == 0:
            pl.semaphore_wait(barrier, devices - 1)
        sent = []
        for d in range(1, n_seq):
            peer = lax.rem(me_s + d, n_seq)
            copy = pltpu.make_async_remote_copy(
                src_ref=qkv_out.at[j, peer],
                dst_ref=qkv_in.at[j, :, me_s],
                send_sem=qkv_send.at[j, d],
                recv_sem=qkv_recv.at[j, d],
                device_id=(me_e, peer),
                device_id_type=MESH,
            )
            copy.start()
            sent.append(copy)
        own = pltpu.make_async_copy(qkv_out.at[j, me_s], qkv_in.at[j, :, me_s], qkv_own.at[j])
        own.start()
        qkv_copies.append((sent, own))

    row_ids = lax.broadcasted_iota(jnp.int32, (slots, toks), 0)
    col_ids = lax.broadcasted_iota(jnp.int32, (toks, slots), 1)
    row_pos = jnp.full((slots, toks), -1, jnp.int32)
    col_pos = jnp.full((toks, slots), -1, jnp.int32)
    for e in range(n_exp):
        for c in range(cap):
            pos = jnp.where(c < counts_ref[0, e], picked_ref[e, c] - me_s * toks, -1)
            row_pos = jnp.where(row_ids == e * cap + c, pos, row_pos)
            col_pos = jnp.where(col_ids == e * cap + c, pos, col_pos)
    pick_rows = row_pos == lax.broadcasted_iota(jnp.int32, (slots, toks), 1)
    pick_cols = col_pos == lax.broadcasted_iota(jnp.int32, (toks, slots), 0)
    pick_rows = jnp.where(pick_rows, 1.0, 0.0).astype(BF)
    pick_cols = jnp.where(pick_cols, 1.0, 0.0)

    score_scale = 1.0 / math.sqrt(head)
    group = min(512 // toks, n_seq)
    att_copies = []
    for j in range(local_heads):
        sent, own = qkv_copies[j]
        own.wait()
        for copy in sent:
            copy.wait_recv()

        def attend(b, carry, j=j):
            at = pl.ds(b * group, group)
            queries = qkv_in[j, 0, at].reshape(group * toks, head)
            keys = qkv_in[j, 1].reshape(length, head)
            values = qkv_in[j, 2].reshape(length, head)
            scores = lax.dot_general(
                queries, keys, (((1,), (1,)), ((), ())), preferred_element_type=F32
            )
            scores = scores * score_scale
            weights = jnp.exp(scores - jnp.max(scores, axis=-1, keepdims=True))
            weights = weights * (1.0 / jnp.sum(weights, axis=-1, keepdims=True))
            mixed = jnp.dot(weights.astype(BF), values, preferred_element_type=F32)
            att_out[j, at] = mixed.astype(BF).reshape(group, toks, head)
            return carry

        if n_seq == group:
            attend(0, 0)
        else:
            lax.fori_loop(0, n_seq // group, attend, 0)
        sent = []
        for d in range(1, n_seq):
            peer = lax.rem(me_s + d, n_seq)
            copy = pltpu.make_async_remote_copy(
                src_ref=att_out.at[j, peer],
                dst_ref=att_in.at[j, me_s],
                send_sem=att_send.at[j, d],
                recv_sem=att_recv.at[j, d],
                device_id=(me_e, peer),
                device_id_type=MESH,
            )
            copy.start()
            sent.append(copy)
        own = pltpu.make_async_copy(att_out.at[j, me_s], att_in.at[j, me_s], att_own.at[j])
        own.start()
        att_copies.append((sent, own))

    for load in loads[1:]:
        load.wait()
    for j in range(local_heads):
        sent, own = att_copies[j]
        own.wait()
        for copy in sent:
            copy.wait_recv()
        for s in range(n_seq):
            first = (s * local_heads + j) * head
            at = slice(first, first + head)
            resid[:, at] = hidden_in[:, at].astype(F32) + mod[0:1, at] * att_in[j, s].astype(F32)

    residual = resid[...]
    centred = residual - jnp.mean(residual, axis=-1, keepdims=True)
    variance = jnp.mean(centred * centred, axis=-1, keepdims=True)
    normed = centred * lax.rsqrt(variance + epsilon_norm)
    modulated = (normed * (1.0 + mod[2:3, :]) + mod[1:2, :]).astype(BF)

    picked_rows = jnp.dot(pick_rows, modulated, preferred_element_type=F32)
    for k in range(pieces):
        stage[pl.ds(k, slots, stride=pieces), :] = picked_rows[:, k * head : (k + 1) * head]
    rows_out[...] = stage[0 : slots * pieces, :].reshape(rows_out.shape).astype(BF)

    def send_rows(d, carry):
        peer_e, peer_s = peer_of(d)
        pltpu.make_async_remote_copy(
            src_ref=rows_out.at[peer_e],
            dst_ref=rows_in.at[me],
            send_sem=row_send,
            recv_sem=row_recv,
            device_id=(peer_e, peer_s),
            device_id_type=MESH,
        ).start()
        return carry

    lax.fori_loop(1, devices, send_rows, 0)
    pltpu.make_async_copy(rows_out.at[me_e], rows_in.at[me], row_recv).start()

    gates = jax.nn.sigmoid(jnp.dot(modulated, router[...], preferred_element_type=F32))
    gate_cols = jnp.zeros((toks, slots), F32)
    for e in range(n_exp):
        gate_cols = jnp.where(col_ids // cap == e, gates[:, e : e + 1], gate_cols)
    gate_cols = gate_cols * pick_cols
    gate_high = gate_cols.astype(BF)
    gate_low = (gate_cols - gate_high.astype(F32)).astype(BF)

    pltpu.make_async_copy(rows_in, rows_in, row_recv).wait()

    block = rows_x.shape[0]
    sources = block // cap

    def apply_expert(b, carry):
        at = pl.ds(b * sources, sources)
        stage[0 : block * pieces, :] = rows_in[at].astype(F32).reshape(block * pieces, head)
        for k in range(pieces):
            rows_x[:, k * head : (k + 1) * head] = stage[
                pl.ds(k, block, stride=pieces), :
            ].astype(BF)
        product = jnp.dot(rows_x[...], win[...], preferred_element_type=F32)
        units = jax.nn.gelu(product, approximate=True).astype(BF)
        partial = jnp.dot(units, wout[...], preferred_element_type=F32)
        for k in range(pieces):
            stage[pl.ds(k, block, stride=pieces), :] = partial[:, k * head : (k + 1) * head]
        ret_out[at] = stage[0 : block * pieces, :].reshape(sources, cap * pieces, head).astype(BF)
        return carry

    if devices == sources:
        apply_expert(0, 0)
    else:
        lax.fori_loop(0, devices // sources, apply_expert, 0)

    def send_back(d, carry):
        peer_e, peer_s = peer_of(d)
        pltpu.make_async_remote_copy(
            src_ref=ret_out.at[peer_e * n_seq + peer_s],
            dst_ref=ret_in.at[me],
            send_sem=ret_send,
            recv_sem=ret_recv,
            device_id=(peer_e, peer_s),
            device_id_type=MESH,
        ).start()
        return carry

    lax.fori_loop(1, devices, send_back, 0)
    pltpu.make_async_copy(ret_out.at[me], ret_in.at[me], ret_recv).start()

    for sent, _ in qkv_copies + att_copies:
        for copy in sent:
            copy.wait_send()
    others = rows_in.at[pl.ds(0, devices - 1)]
    pltpu.make_async_copy(others, others, row_send).wait()

    pltpu.make_async_copy(ret_in, ret_in, ret_recv).wait()
    for e in range(n_exp):
        summed = jnp.sum(ret_in[e * n_seq : (e + 1) * n_seq].astype(F32), axis=0)
        stage[e * cap * pieces : (e + 1) * cap * pieces, :] = summed
    for k in range(pieces):
        rows_e[:, k * head : (k + 1) * head] = stage[pl.ds(k, slots, stride=pieces), :].astype(BF)
    expert_rows = rows_e[...]
    mixture = jnp.dot(gate_high, expert_rows, preferred_element_type=F32) + jnp.dot(
        gate_low, expert_rows, preferred_element_type=F32
    )
    out_ref[...] = (resid[...] + mod[3:4, :] * mixture).astype(BF)

    others = ret_in.at[pl.ds(0, devices - 1)]
    pltpu.make_async_copy(others, others, ret_send).wait()


def per_device(
    n_exp, n_seq, projected, hidden_in, modulation, w_router, picked, counts, weight_in, weight_out
):
    _, toks, three, heads, head = projected.shape
    width = hidden_in.shape[2]
    units = weight_in.shape[2]
    experts = w_router.shape[1]
    cap = picked.shape[3]
    devices = n_exp * n_seq
    slots = experts * cap
    pieces = width // head
    local_heads = heads // n_seq
    block = min(64, devices * cap)
    dma = pltpu.SemaphoreType.DMA
    anywhere = pl.BlockSpec(memory_space=pl.ANY)
    scalars = pl.BlockSpec(memory_space=pltpu.SMEM)
    rows = toks * three * heads
    flops = (
        4 * local_heads * (toks * n_seq) ** 2 * head + 4 * devices * cap * width * units
    )
    out = pl.pallas_call(
        functools.partial(block_kernel, n_exp, n_seq, heads, cap),
        out_shape=jax.ShapeDtypeStruct((toks, width), BF),
        in_specs=[scalars] * 2 + [anywhere] * 6,
        out_specs=pl.BlockSpec(memory_space=pltpu.VMEM),
        scratch_shapes=[
            pltpu.VMEM((rows, head), BF),
            pltpu.VMEM((toks, width), BF),
            pltpu.VMEM((4, width), F32),
            pltpu.VMEM((width, experts), BF),
            pltpu.VMEM((width, units), BF),
            pltpu.VMEM((units, width), BF),
            pltpu.VMEM((rows, head), F32),
            pltpu.VMEM((local_heads, n_seq, three, toks, head), BF),
            pltpu.VMEM((local_heads, three, n_seq, toks, head), BF),
            pltpu.VMEM((local_heads, n_seq, toks, head), BF),
            pltpu.VMEM((local_heads, n_seq, toks, head), BF),
            pltpu.VMEM((toks, width), F32),
            pltpu.VMEM((max(block, slots) * pieces, head), F32),
            pltpu.VMEM((experts, cap * pieces, head), BF),
            pltpu.VMEM((devices, cap * pieces, head), BF),
            pltpu.VMEM((block, width), BF),
            pltpu.VMEM((devices, cap * pieces, head), BF),
            pltpu.VMEM((devices, cap * pieces, head), BF),
            pltpu.VMEM((slots, width), BF),
            dma((6,)),
            dma((local_heads, n_seq)),
            dma((local_heads, n_seq)),
            dma((local_heads,)),
            dma((local_heads, n_seq)),
            dma((local_heads, n_seq)),
            dma((local_heads,)),
            dma,
            dma,
            dma,
            dma,
        ],
        compiler_params=pltpu.CompilerParams(
            collective_id=0, has_side_effects=True, vmem_limit_bytes=56 * 1024 * 1024
        ),
        cost_estimate=pl.CostEstimate(
            flops=flops, bytes_accessed=4 * width * units, transcendentals=0
        ),
    )(
        picked.reshape(experts, cap),
        counts.reshape(1, experts),
        projected.reshape(rows, head),
        hidden_in[0],
        modulation[0],
        w_router,
        weight_in[0],
        weight_out[0],
    )
    return out[None]


def solution(mesh):
    in_specs = (
        P("exp", "seq", None, None, None),
        P("exp", "seq", None),
        P("exp", None, None),
        P(),
        P("exp", "seq", None, None),
        P("exp", "seq", None),
        P("exp", None, "seq"),
        P("exp", "seq", None),
    )
    out_specs = P("exp", "seq", None)
    return jax.shard_map(
        functools.partial(per_device, mesh.shape["exp"], mesh.shape["seq"]),
        mesh=mesh,
        in_specs=in_specs,
        out_specs=out_specs,
        check_vma=False,
    )
```

```python
import functools
import math

import jax
import jax.numpy as jnp
from jax import lax
from jax.experimental import pallas as pl
from jax.experimental.pallas import tpu as pltpu
from jax.sharding import PartitionSpec as P

epsilon_norm = 1e-06
MESH = pl.DeviceIdType.MESH
BF = jnp.bfloat16
F32 = jnp.float32


def block_kernel(
    n_exp,
    n_seq,
    heads,
    cap,
    picked_ref,
    counts_ref,
    proj_hbm,
    hidden_hbm,
    mod_hbm,
    router_hbm,
    win_hbm,
    wout_hbm,
    out_ref,
    proj,
    hidden_in,
    mod,
    router,
    win,
    wout,
    wide,
    qkv_out,
    qkv_in,
    att_out,
    att_in,
    resid,
    stage,
    rows_out,
    rows_in,
    rows_x,
    ret_out,
    ret_in,
    rows_e,
    load_sem,
    qkv_send,
    qkv_recv,
    qkv_own,
    att_send,
    att_recv,
    att_own,
    row_send,
    row_recv,
    ret_send,
    ret_recv,
):
    me_e = lax.axis_index("exp")
    me_s = lax.axis_index("seq")
    devices = n_exp * n_seq
    toks = hidden_in.shape[0]
    width = hidden_in.shape[1]
    head = proj.shape[1]
    local_heads = heads // n_seq
    length = toks * n_seq
    slots = n_exp * cap
    pieces = width // head
    me = me_e * n_seq + me_s

    offsets = list(range(n_seq // 2, n_seq)) + list(range(n_seq // 2 - 1, -1, -1))

    def to_all(send):
        for ds in offsets:

            def step(de, carry, ds=ds):
                send(lax.rem(me_e + de, n_exp), lax.rem(me_s + ds, n_seq))
                return carry

            lax.fori_loop(0 if ds else 1, n_exp, step, 0)

    barrier = pltpu.get_barrier_semaphore()
    greeted = n_seq - 1 + n_exp - 1
    for d in range(1, n_seq):
        peer = (me_e, lax.rem(me_s + d, n_seq))
        pl.semaphore_signal(barrier, inc=1, device_id=peer, device_id_type=MESH)
    for d in range(1, n_exp):
        peer = (lax.rem(me_e + d, n_exp), me_s)
        pl.semaphore_signal(barrier, inc=1, device_id=peer, device_id_type=MESH)

    loads = [
        pltpu.make_async_copy(src, dst, load_sem.at[i])
        for i, (src, dst) in enumerate(
            (
                (proj_hbm, proj),
                (hidden_hbm, hidden_in),
                (mod_hbm, mod),
                (router_hbm, router),
                (win_hbm, win),
                (wout_hbm, wout),
            )
        )
    ]
    for load in loads:
        load.start()

    loads[0].wait()
    wide[...] = proj[...].astype(F32)
    qkv_copies = []
    for j in range(local_heads):
        for s in range(n_seq):
            for c in range(3):
                first = c * heads + s * local_heads + j
                qkv_out[j, s, c] = wide[pl.ds(first, toks, stride=3 * heads), :].astype(BF)
        if j == 0:
            pl.semaphore_wait(barrier, greeted)
        sent = []
        for d in range(1, n_seq):
            peer = lax.rem(me_s + d, n_seq)
            copy = pltpu.make_async_remote_copy(
                src_ref=qkv_out.at[j, peer],
                dst_ref=qkv_in.at[j, :, me_s],
                send_sem=qkv_send.at[j, d],
                recv_sem=qkv_recv.at[j, d],
                device_id=(me_e, peer),
                device_id_type=MESH,
            )
            copy.start()
            sent.append(copy)
        own = pltpu.make_async_copy(qkv_out.at[j, me_s], qkv_in.at[j, :, me_s], qkv_own.at[j])
        own.start()
        qkv_copies.append((sent, own))

    row_ids = lax.broadcasted_iota(jnp.int32, (slots, toks), 0)
    col_ids = lax.broadcasted_iota(jnp.int32, (toks, slots), 1)
    row_pos = jnp.full((slots, toks), -1, jnp.int32)
    col_pos = jnp.full((toks, slots), -1, jnp.int32)
    for e in range(n_exp):
        for c in range(cap):
            pos = jnp.where(c < counts_ref[0, e], picked_ref[c, e] - me_s * toks, -1)
            row_pos = jnp.where(row_ids == e * cap + c, pos, row_pos)
            col_pos = jnp.where(col_ids == e * cap + c, pos, col_pos)
    pick_rows = row_pos == lax.broadcasted_iota(jnp.int32, (slots, toks), 1)
    pick_cols = col_pos == lax.broadcasted_iota(jnp.int32, (toks, slots), 0)
    pick_rows = jnp.where(pick_rows, 1.0, 0.0).astype(BF)
    pick_cols = jnp.where(pick_cols, 1.0, 0.0)

    score_scale = 1.0 / math.sqrt(head)
    group = min(512 // toks, n_seq)
    att_copies = []
    for j in range(local_heads):
        sent, own = qkv_copies[j]
        own.wait()
        for copy in sent:
            copy.wait_recv()

        def attend(b, carry, j=j):
            at = pl.ds(b * group, group)
            queries = qkv_in[j, 0, at].reshape(group * toks, head)
            keys = qkv_in[j, 1].reshape(length, head)
            values = qkv_in[j, 2].reshape(length, head)
            scores = lax.dot_general(
                queries, keys, (((1,), (1,)), ((), ())), preferred_element_type=F32
            )
            scores = scores * score_scale
            weights = jnp.exp(scores - jnp.max(scores, axis=-1, keepdims=True))
            weights = weights * (1.0 / jnp.sum(weights, axis=-1, keepdims=True))
            mixed = jnp.dot(weights.astype(BF), values, preferred_element_type=F32)
            att_out[j, at] = mixed.astype(BF).reshape(group, toks, head)
            return carry

        if n_seq == group:
            attend(0, 0)
        else:
            lax.fori_loop(0, n_seq // group, attend, 0)
        sent = []
        for d in range(1, n_seq):
            peer = lax.rem(me_s + d, n_seq)
            copy = pltpu.make_async_remote_copy(
                src_ref=att_out.at[j, peer],
                dst_ref=att_in.at[j, me_s],
                send_sem=att_send.at[j, d],
                recv_sem=att_recv.at[j, d],
                device_id=(me_e, peer),
                device_id_type=MESH,
            )
            copy.start()
            sent.append(copy)
        own = pltpu.make_async_copy(att_out.at[j, me_s], att_in.at[j, me_s], att_own.at[j])
        own.start()
        att_copies.append((sent, own))

    for load in loads[1:]:
        load.wait()
    for j in range(local_heads):
        sent, own = att_copies[j]
        own.wait()
        for copy in sent:
            copy.wait_recv()
        for s in range(n_seq):
            first = (s * local_heads + j) * head
            at = slice(first, first + head)
            resid[:, at] = hidden_in[:, at].astype(F32) + mod[0:1, at] * att_in[j, s].astype(F32)

    residual = resid[...]
    centred = residual - jnp.mean(residual, axis=-1, keepdims=True)
    variance = jnp.mean(centred * centred, axis=-1, keepdims=True)
    normed = centred * lax.rsqrt(variance + epsilon_norm)
    modulated = (normed * (1.0 + mod[2:3, :]) + mod[1:2, :]).astype(BF)

    picked_rows = jnp.dot(pick_rows, modulated, preferred_element_type=F32)
    for k in range(pieces):
        stage[pl.ds(k, slots, stride=pieces), :] = picked_rows[:, k * head : (k + 1) * head]
    rows_out[...] = stage[0 : slots * pieces, :].reshape(rows_out.shape).astype(BF)

    def send_rows(peer_e, peer_s):
        pltpu.make_async_remote_copy(
            src_ref=rows_out.at[peer_e],
            dst_ref=rows_in.at[me],
            send_sem=row_send,
            recv_sem=row_recv,
            device_id=(peer_e, peer_s),
            device_id_type=MESH,
        ).start()

    to_all(send_rows)
    pltpu.make_async_copy(rows_out.at[me_e], rows_in.at[me], row_recv).start()

    gates = jax.nn.sigmoid(
        lax.dot_general(
            modulated, router[...], (((1,), (1,)), ((), ())), preferred_element_type=F32
        )
    )
    gate_cols = jnp.zeros((toks, slots), F32)
    for e in range(n_exp):
        gate_cols = jnp.where(col_ids // cap == e, gates[:, e : e + 1], gate_cols)
    gate_cols = gate_cols * pick_cols
    gate_high = gate_cols.astype(BF)
    gate_low = (gate_cols - gate_high.astype(F32)).astype(BF)

    pltpu.make_async_copy(rows_in, rows_in, row_recv).wait()

    block = rows_x.shape[0]
    sources = block // cap

    def apply_expert(b, carry):
        at = pl.ds(b * sources, sources)
        stage[0 : block * pieces, :] = rows_in[at].astype(F32).reshape(block * pieces, head)
        for k in range(pieces):
            rows_x[:, k * head : (k + 1) * head] = stage[
                pl.ds(k, block, stride=pieces), :
            ].astype(BF)
        product = jnp.dot(rows_x[...], win[...], preferred_element_type=F32)
        units = jax.nn.gelu(product, approximate=True).astype(BF)
        partial = jnp.dot(units, wout[...], preferred_element_type=F32)
        for k in range(pieces):
            stage[pl.ds(k, block, stride=pieces), :] = partial[:, k * head : (k + 1) * head]
        ret_out[at] = stage[0 : block * pieces, :].reshape(sources, cap * pieces, head).astype(BF)
        return carry

    if devices == sources:
        apply_expert(0, 0)
    else:
        lax.fori_loop(0, devices // sources, apply_expert, 0)

    def send_back(peer_e, peer_s):
        pltpu.make_async_remote_copy(
            src_ref=ret_out.at[peer_e * n_seq + peer_s],
            dst_ref=ret_in.at[me],
            send_sem=ret_send,
            recv_sem=ret_recv,
            device_id=(peer_e, peer_s),
            device_id_type=MESH,
        ).start()

    to_all(send_back)
    pltpu.make_async_copy(ret_out.at[me], ret_in.at[me], ret_recv).start()

    for sent, _ in qkv_copies + att_copies:
        for copy in sent:
            copy.wait_send()
    others = rows_in.at[pl.ds(0, devices - 1)]
    pltpu.make_async_copy(others, others, row_send).wait()

    pltpu.make_async_copy(ret_in, ret_in, ret_recv).wait()
    for e in range(n_exp):
        summed = jnp.sum(ret_in[e * n_seq : (e + 1) * n_seq].astype(F32), axis=0)
        stage[e * cap * pieces : (e + 1) * cap * pieces, :] = summed
    for k in range(pieces):
        rows_e[:, k * head : (k + 1) * head] = stage[pl.ds(k, slots, stride=pieces), :].astype(BF)
    expert_rows = rows_e[...]
    mixture = jnp.dot(gate_high, expert_rows, preferred_element_type=F32) + jnp.dot(
        gate_low, expert_rows, preferred_element_type=F32
    )
    out_ref[...] = (resid[...] + mod[3:4, :] * mixture).astype(BF)

    others = ret_in.at[pl.ds(0, devices - 1)]
    pltpu.make_async_copy(others, others, ret_send).wait()


def per_device(
    n_exp, n_seq, projected, hidden_in, modulation, w_router, picked, counts, weight_in, weight_out
):
    _, toks, three, heads, head = projected.shape
    width = hidden_in.shape[2]
    units = weight_in.shape[2]
    experts = w_router.shape[1]
    cap = picked.shape[3]
    devices = n_exp * n_seq
    slots = experts * cap
    pieces = width // head
    local_heads = heads // n_seq
    block = min(64, devices * cap)
    dma = pltpu.SemaphoreType.DMA
    anywhere = pl.BlockSpec(memory_space=pl.ANY)
    scalars = pl.BlockSpec(memory_space=pltpu.SMEM)
    rows = toks * three * heads
    flops = (
        4 * local_heads * (toks * n_seq) ** 2 * head + 4 * devices * cap * width * units
    )
    out = pl.pallas_call(
        functools.partial(block_kernel, n_exp, n_seq, heads, cap),
        out_shape=jax.ShapeDtypeStruct((toks, width), BF),
        in_specs=[scalars] * 2 + [anywhere] * 6,
        out_specs=pl.BlockSpec(memory_space=pltpu.VMEM),
        scratch_shapes=[
            pltpu.VMEM((rows, head), BF),
            pltpu.VMEM((toks, width), BF),
            pltpu.VMEM((4, width), F32),
            pltpu.VMEM((experts, width), BF),
            pltpu.VMEM((width, units), BF),
            pltpu.VMEM((units, width), BF),
            pltpu.VMEM((rows, head), F32),
            pltpu.VMEM((local_heads, n_seq, three, toks, head), BF),
            pltpu.VMEM((local_heads, three, n_seq, toks, head), BF),
            pltpu.VMEM((local_heads, n_seq, toks, head), BF),
            pltpu.VMEM((local_heads, n_seq, toks, head), BF),
            pltpu.VMEM((toks, width), F32),
            pltpu.VMEM((max(block, slots) * pieces, head), F32),
            pltpu.VMEM((experts, cap * pieces, head), BF),
            pltpu.VMEM((devices, cap * pieces, head), BF),
            pltpu.VMEM((block, width), BF),
            pltpu.VMEM((devices, cap * pieces, head), BF),
            pltpu.VMEM((devices, cap * pieces, head), BF),
            pltpu.VMEM((slots, width), BF),
            dma((6,)),
            dma((local_heads, n_seq)),
            dma((local_heads, n_seq)),
            dma((local_heads,)),
            dma((local_heads, n_seq)),
            dma((local_heads, n_seq)),
            dma((local_heads,)),
            dma,
            dma,
            dma,
            dma,
        ],
        compiler_params=pltpu.CompilerParams(
            collective_id=0, has_side_effects=True, vmem_limit_bytes=56 * 1024 * 1024
        ),
        cost_estimate=pl.CostEstimate(
            flops=flops, bytes_accessed=4 * width * units, transcendentals=0
        ),
    )(
        picked.reshape(experts, cap).T,
        counts.reshape(1, experts),
        projected.reshape(rows, head),
        hidden_in[0],
        modulation[0],
        w_router.T,
        weight_in[0],
        weight_out[0],
    )
    return out[None]


def solution(mesh):
    in_specs = (
        P("exp", "seq", None, None, None),
        P("exp", "seq", None),
        P("exp", None, None),
        P(),
        P("exp", "seq", None, None),
        P("exp", "seq", None),
        P("exp", None, "seq"),
        P("exp", "seq", None),
    )
    out_specs = P("exp", "seq", None)
    return jax.shard_map(
        functools.partial(per_device, mesh.shape["exp"], mesh.shape["seq"]),
        mesh=mesh,
        in_specs=in_specs,
        out_specs=out_specs,
        check_vma=False,
    )
```

```python
import functools
import math

import jax
import jax.numpy as jnp
from jax import lax
from jax.experimental import pallas as pl
from jax.experimental.pallas import tpu as pltpu
from jax.sharding import PartitionSpec as P

epsilon_norm = 1e-06
MESH = pl.DeviceIdType.MESH
BF = jnp.bfloat16
F32 = jnp.float32


def block_kernel(
    n_exp,
    n_seq,
    heads,
    cap,
    picked_hbm,
    counts_hbm,
    proj_hbm,
    hidden_hbm,
    mod_hbm,
    router_hbm,
    win_hbm,
    wout_hbm,
    out_ref,
    picked_ref,
    counts_ref,
    proj,
    hidden_in,
    mod,
    router,
    win,
    wout,
    wide,
    qkv_out,
    qkv_in,
    att_out,
    att_in,
    resid,
    stage,
    rows_out,
    rows_in,
    rows_x,
    ret_out,
    ret_in,
    rows_e,
    load_sem,
    qkv_send,
    qkv_recv,
    qkv_own,
    att_send,
    att_recv,
    att_own,
    row_send,
    row_recv,
    ret_send,
    ret_recv,
):
    me_e = lax.axis_index("exp")
    me_s = lax.axis_index("seq")
    devices = n_exp * n_seq
    toks = hidden_in.shape[0]
    width = hidden_in.shape[1]
    head = proj.shape[1]
    local_heads = heads // n_seq
    length = toks * n_seq
    slots = n_exp * cap
    pieces = width // head
    me = me_e * n_seq + me_s

    offsets = list(range(n_seq // 2, n_seq)) + list(range(n_seq // 2 - 1, -1, -1))

    def to_all(send):
        for ds in offsets:

            def step(de, carry, ds=ds):
                send(lax.rem(me_e + de, n_exp), lax.rem(me_s + ds, n_seq))
                return carry

            lax.fori_loop(0 if ds else 1, n_exp, step, 0)

    barrier = pltpu.get_barrier_semaphore()
    greeted = n_seq - 1 + n_exp - 1
    for d in range(1, n_seq):
        peer = (me_e, lax.rem(me_s + d, n_seq))
        pl.semaphore_signal(barrier, inc=1, device_id=peer, device_id_type=MESH)
    for d in range(1, n_exp):
        peer = (lax.rem(me_e + d, n_exp), me_s)
        pl.semaphore_signal(barrier, inc=1, device_id=peer, device_id_type=MESH)

    loads = [
        pltpu.make_async_copy(src, dst, load_sem.at[i])
        for i, (src, dst) in enumerate(
            (
                (proj_hbm, proj),
                (hidden_hbm, hidden_in),
                (mod_hbm, mod),
                (router_hbm, router),
                (win_hbm, win),
                (wout_hbm, wout),
                (picked_hbm, picked_ref),
                (counts_hbm, counts_ref),
            )
        )
    ]
    for load in loads:
        load.start()

    loads[0].wait()
    wide[...] = proj[...].astype(F32)
    qkv_copies = []
    for j in range(local_heads):
        for s in range(n_seq):
            for c in range(3):
                first = c * heads + s * local_heads + j
                qkv_out[j, s, c] = wide[pl.ds(first, toks, stride=3 * heads), :].astype(BF)
        if j == 0:
            pl.semaphore_wait(barrier, greeted)
        sent = []
        for d in range(1, n_seq):
            peer = lax.rem(me_s + d, n_seq)
            copy = pltpu.make_async_remote_copy(
                src_ref=qkv_out.at[j, peer],
                dst_ref=qkv_in.at[j, :, me_s],
                send_sem=qkv_send.at[j, d],
                recv_sem=qkv_recv.at[j, d],
                device_id=(me_e, peer),
                device_id_type=MESH,
            )
            copy.start()
            sent.append(copy)
        own = pltpu.make_async_copy(qkv_out.at[j, me_s], qkv_in.at[j, :, me_s], qkv_own.at[j])
        own.start()
        qkv_copies.append((sent, own))

    for load in loads[6:]:
        load.wait()

    row_ids = lax.broadcasted_iota(jnp.int32, (slots, toks), 0)
    col_ids = lax.broadcasted_iota(jnp.int32, (toks, slots), 1)
    row_pos = jnp.full((slots, toks), -1, jnp.int32)
    col_pos = jnp.full((toks, slots), -1, jnp.int32)
    for e in range(n_exp):
        for c in range(cap):
            pos = jnp.where(c < counts_ref[0, e], picked_ref[c, e] - me_s * toks, -1)
            row_pos = jnp.where(row_ids == e * cap + c, pos, row_pos)
            col_pos = jnp.where(col_ids == e * cap + c, pos, col_pos)
    pick_rows = row_pos == lax.broadcasted_iota(jnp.int32, (slots, toks), 1)
    pick_cols = col_pos == lax.broadcasted_iota(jnp.int32, (toks, slots), 0)
    pick_rows = jnp.where(pick_rows, 1.0, 0.0).astype(BF)
    pick_cols = jnp.where(pick_cols, 1.0, 0.0)

    score_scale = 1.0 / math.sqrt(head)
    group = min(512 // toks, n_seq)
    att_copies = []

    def send_back_heads(j):
        sent = []
        for d in range(1, n_seq):
            peer = lax.rem(me_s + d, n_seq)
            copy = pltpu.make_async_remote_copy(
                src_ref=att_out.at[j, peer],
                dst_ref=att_in.at[j, me_s],
                send_sem=att_send.at[j, d],
                recv_sem=att_recv.at[j, d],
                device_id=(me_e, peer),
                device_id_type=MESH,
            )
            copy.start()
            sent.append(copy)
        own = pltpu.make_async_copy(att_out.at[j, me_s], att_in.at[j, me_s], att_own.at[j])
        own.start()
        att_copies.append((sent, own))

    for j in range(local_heads):
        sent, own = qkv_copies[j]
        if 0 < j == local_heads - 1:
            for copy in sent:
                copy.wait_send()
            for earlier in range(j):
                send_back_heads(earlier)
        own.wait()
        for copy in sent:
            copy.wait_recv()

        def attend(b, carry, j=j):
            at = pl.ds(b * group, group)
            queries = qkv_in[j, 0, at].reshape(group * toks, head)
            keys = qkv_in[j, 1].reshape(length, head)
            values = qkv_in[j, 2].reshape(length, head)
            scores = lax.dot_general(
                queries, keys, (((1,), (1,)), ((), ())), preferred_element_type=F32
            )
            scores = scores * score_scale
            weights = jnp.exp(scores - jnp.max(scores, axis=-1, keepdims=True))
            weights = weights * (1.0 / jnp.sum(weights, axis=-1, keepdims=True))
            mixed = jnp.dot(weights.astype(BF), values, preferred_element_type=F32)
            att_out[j, at] = mixed.astype(BF).reshape(group, toks, head)
            return carry

        if n_seq == group:
            attend(0, 0)
        else:
            lax.fori_loop(0, n_seq // group, attend, 0)
    send_back_heads(local_heads - 1)

    for load in loads[1:6]:
        load.wait()
    for j in range(local_heads):
        sent, own = att_copies[j]
        own.wait()
        for copy in sent:
            copy.wait_recv()
        for s in range(n_seq):
            first = (s * local_heads + j) * head
            at = slice(first, first + head)
            resid[:, at] = hidden_in[:, at].astype(F32) + mod[0:1, at] * att_in[j, s].astype(F32)

    residual = resid[...]
    centred = residual - jnp.mean(residual, axis=-1, keepdims=True)
    variance = jnp.mean(centred * centred, axis=-1, keepdims=True)
    normed = centred * lax.rsqrt(variance + epsilon_norm)
    modulated = (normed * (1.0 + mod[2:3, :]) + mod[1:2, :]).astype(BF)

    parts = rows_in.shape[0]
    depth = pieces // parts

    def columns(part, k):
        return slice((part * depth + k) * head, (part * depth + k + 1) * head)

    def part_columns(part):
        return slice(part * depth * head, (part + 1) * depth * head)

    picked_rows = jnp.dot(pick_rows, modulated, preferred_element_type=F32)
    for part in range(parts):
        for k in range(depth):
            stage[pl.ds(k, slots, stride=depth), :] = picked_rows[:, columns(part, k)]
        rows_out[part] = stage[0 : slots * depth, :].reshape(rows_out.shape[1:]).astype(BF)

        def send_rows(peer_e, peer_s, part=part):
            pltpu.make_async_remote_copy(
                src_ref=rows_out.at[part, peer_e],
                dst_ref=rows_in.at[part, me],
                send_sem=row_send.at[part],
                recv_sem=row_recv.at[part],
                device_id=(peer_e, peer_s),
                device_id_type=MESH,
            ).start()

        to_all(send_rows)
        pltpu.make_async_copy(
            rows_out.at[part, me_e], rows_in.at[part, me], row_recv.at[part]
        ).start()

    gates = jax.nn.sigmoid(
        lax.dot_general(
            modulated, router[...], (((1,), (1,)), ((), ())), preferred_element_type=F32
        )
    )
    gate_cols = jnp.zeros((toks, slots), F32)
    for e in range(n_exp):
        gate_cols = jnp.where(col_ids // cap == e, gates[:, e : e + 1], gate_cols)
    gate_cols = gate_cols * pick_cols
    gate_high = gate_cols.astype(BF)
    gate_low = (gate_cols - gate_high.astype(F32)).astype(BF)

    block = rows_x.shape[0]
    sources = block // cap
    single = devices == sources

    def rows_arrive(part):
        pltpu.make_async_copy(rows_in.at[part], rows_in.at[part], row_recv.at[part]).wait()

    def send_part(part):
        def send_back(peer_e, peer_s):
            pltpu.make_async_remote_copy(
                src_ref=ret_out.at[part, peer_e * n_seq + peer_s],
                dst_ref=ret_in.at[part, me],
                send_sem=ret_send.at[part],
                recv_sem=ret_recv.at[part],
                device_id=(peer_e, peer_s),
                device_id_type=MESH,
            ).start()

        to_all(send_back)
        pltpu.make_async_copy(
            ret_out.at[part, me], ret_in.at[part, me], ret_recv.at[part]
        ).start()

    def apply_expert(b, carry):
        at = pl.ds(b * sources, sources)
        product = jnp.zeros((block, win.shape[1]), F32)
        for part in range(parts):
            if single:
                rows_arrive(part)
            stage[0 : block * depth, :] = (
                rows_in[part, at].astype(F32).reshape(block * depth, head)
            )
            for k in range(depth):
                rows_x[:, columns(part, k)] = stage[pl.ds(k, block, stride=depth), :].astype(BF)
            span = part_columns(part)
            product += jnp.dot(rows_x[:, span], win[span, :], preferred_element_type=F32)
        units = jax.nn.gelu(product, approximate=True).astype(BF)
        for part in range(parts):
            partial = jnp.dot(units, wout[:, part_columns(part)], preferred_element_type=F32)
            for k in range(depth):
                stage[pl.ds(k, block, stride=depth), :] = partial[:, k * head : (k + 1) * head]
            ret_out[part, at] = (
                stage[0 : block * depth, :].reshape(sources, cap * depth, head).astype(BF)
            )
            if single:
                send_part(part)
        return carry

    if single:
        apply_expert(0, 0)
    else:
        for part in range(parts):
            rows_arrive(part)
        lax.fori_loop(0, devices // sources, apply_expert, 0)
        for part in range(parts):
            send_part(part)

    for j in range(local_heads):
        if not 0 < j == local_heads - 1:
            for copy in qkv_copies[j][0]:
                copy.wait_send()
        for copy in att_copies[j][0]:
            copy.wait_send()
    for part in range(parts):
        others = rows_in.at[part, pl.ds(0, devices - 1)]
        pltpu.make_async_copy(others, others, row_send.at[part]).wait()

    for part in range(parts):
        pltpu.make_async_copy(ret_in.at[part], ret_in.at[part], ret_recv.at[part]).wait()
        for e in range(n_exp):
            summed = jnp.sum(ret_in[part, e * n_seq : (e + 1) * n_seq].astype(F32), axis=0)
            stage[e * cap * depth : (e + 1) * cap * depth, :] = summed
        for k in range(depth):
            rows_e[:, columns(part, k)] = stage[pl.ds(k, slots, stride=depth), :].astype(BF)
        span = part_columns(part)
        expert_rows = rows_e[:, span]
        mixture = jnp.dot(gate_high, expert_rows, preferred_element_type=F32) + jnp.dot(
            gate_low, expert_rows, preferred_element_type=F32
        )
        out_ref[:, span] = (resid[:, span] + mod[3:4, span] * mixture).astype(BF)

    for part in range(parts):
        others = ret_in.at[part, pl.ds(0, devices - 1)]
        pltpu.make_async_copy(others, others, ret_send.at[part]).wait()


def per_device(
    n_exp, n_seq, projected, hidden_in, modulation, w_router, picked, counts, weight_in, weight_out
):
    _, toks, three, heads, head = projected.shape
    width = hidden_in.shape[2]
    units = weight_in.shape[2]
    experts = w_router.shape[1]
    cap = picked.shape[3]
    devices = n_exp * n_seq
    slots = experts * cap
    pieces = width // head
    parts = 1
    depth = pieces // parts
    local_heads = heads // n_seq
    block = min(64, devices * cap)
    dma = pltpu.SemaphoreType.DMA
    anywhere = pl.BlockSpec(memory_space=pl.ANY)
    rows = toks * three * heads
    flops = (
        4 * local_heads * (toks * n_seq) ** 2 * head + 4 * devices * cap * width * units
    )
    out = pl.pallas_call(
        functools.partial(block_kernel, n_exp, n_seq, heads, cap),
        out_shape=jax.ShapeDtypeStruct((toks, width), BF),
        in_specs=[anywhere] * 8,
        out_specs=pl.BlockSpec(memory_space=pltpu.VMEM),
        scratch_shapes=[
            pltpu.SMEM((cap, experts), jnp.int32),
            pltpu.SMEM((1, experts), jnp.int32),
            pltpu.VMEM((rows, head), BF),
            pltpu.VMEM((toks, width), BF),
            pltpu.VMEM((4, width), F32),
            pltpu.VMEM((experts, width), BF),
            pltpu.VMEM((width, units), BF),
            pltpu.VMEM((units, width), BF),
            pltpu.VMEM((rows, head), F32),
            pltpu.VMEM((local_heads, n_seq, three, toks, head), BF),
            pltpu.VMEM((local_heads, three, n_seq, toks, head), BF),
            pltpu.VMEM((local_heads, n_seq, toks, head), BF),
            pltpu.VMEM((local_heads, n_seq, toks, head), BF),
            pltpu.VMEM((toks, width), F32),
            pltpu.VMEM((max(block, slots) * depth, head), F32),
            pltpu.VMEM((parts, experts, cap * depth, head), BF),
            pltpu.VMEM((parts, devices, cap * depth, head), BF),
            pltpu.VMEM((block, width), BF),
            pltpu.VMEM((parts, devices, cap * depth, head), BF),
            pltpu.VMEM((parts, devices, cap * depth, head), BF),
            pltpu.VMEM((slots, width), BF),
            dma((8,)),
            dma((local_heads, n_seq)),
            dma((local_heads, n_seq)),
            dma((local_heads,)),
            dma((local_heads, n_seq)),
            dma((local_heads, n_seq)),
            dma((local_heads,)),
            dma((parts,)),
            dma((parts,)),
            dma((parts,)),
            dma((parts,)),
        ],
        compiler_params=pltpu.CompilerParams(
            collective_id=0, has_side_effects=True, vmem_limit_bytes=56 * 1024 * 1024
        ),
        cost_estimate=pl.CostEstimate(
            flops=flops, bytes_accessed=4 * width * units, transcendentals=0
        ),
    )(
        picked.reshape(experts, cap).T,
        counts.reshape(1, experts),
        projected.reshape(rows, head),
        hidden_in[0],
        modulation[0],
        w_router.T,
        weight_in[0],
        weight_out[0],
    )
    return out[None]


def solution(mesh):
    in_specs = (
        P("exp", "seq", None, None, None),
        P("exp", "seq", None),
        P("exp", None, None),
        P(),
        P("exp", "seq", None, None),
        P("exp", "seq", None),
        P("exp", None, "seq"),
        P("exp", "seq", None),
    )
    out_specs = P("exp", "seq", None)
    return jax.shard_map(
        functools.partial(per_device, mesh.shape["exp"], mesh.shape["seq"]),
        mesh=mesh,
        in_specs=in_specs,
        out_specs=out_specs,
        check_vma=False,
    )
```

```python
import functools
import math

import jax
import jax.numpy as jnp
from jax import lax
from jax.experimental import pallas as pl
from jax.experimental.pallas import tpu as pltpu
from jax.sharding import PartitionSpec as P

epsilon_norm = 1e-06
MESH = pl.DeviceIdType.MESH
BF = jnp.bfloat16
F32 = jnp.float32


def block_kernel(
    n_exp,
    n_seq,
    heads,
    cap,
    picked_hbm,
    counts_hbm,
    proj_hbm,
    hidden_hbm,
    mod_hbm,
    router_hbm,
    win_hbm,
    wout_hbm,
    out_ref,
    picked_ref,
    counts_ref,
    proj,
    hidden_in,
    mod,
    router,
    win,
    wout,
    wide,
    qkv_out,
    qkv_in,
    att_out,
    att_in,
    resid,
    stage,
    rows_out,
    rows_in,
    rows_x,
    ret_out,
    ret_in,
    rows_e,
    load_sem,
    qkv_send,
    qkv_recv,
    qkv_own,
    att_send,
    att_recv,
    att_own,
    row_send,
    row_recv,
    ret_send,
    ret_recv,
):
    me_e = lax.axis_index("exp")
    me_s = lax.axis_index("seq")
    devices = n_exp * n_seq
    toks = hidden_in.shape[0]
    width = hidden_in.shape[1]
    head = proj.shape[1]
    local_heads = heads // n_seq
    length = toks * n_seq
    slots = n_exp * cap
    pieces = width // head
    me = me_e * n_seq + me_s

    offsets = list(range(n_seq // 2, n_seq)) + list(range(n_seq // 2 - 1, -1, -1))

    def to_all(send):
        for ds in offsets:

            def step(de, carry, ds=ds):
                send(lax.rem(me_e + de, n_exp), lax.rem(me_s + ds, n_seq))
                return carry

            lax.fori_loop(0 if ds else 1, n_exp, step, 0)

    barrier = pltpu.get_barrier_semaphore()
    greeted = n_seq - 1 + n_exp - 1
    for d in range(1, n_seq):
        peer = (me_e, lax.rem(me_s + d, n_seq))
        pl.semaphore_signal(barrier, inc=1, device_id=peer, device_id_type=MESH)
    for d in range(1, n_exp):
        peer = (lax.rem(me_e + d, n_exp), me_s)
        pl.semaphore_signal(barrier, inc=1, device_id=peer, device_id_type=MESH)

    loads = [
        pltpu.make_async_copy(src, dst, load_sem.at[i])
        for i, (src, dst) in enumerate(
            (
                (proj_hbm, proj),
                (hidden_hbm, hidden_in),
                (mod_hbm, mod),
                (router_hbm, router),
                (win_hbm, win),
                (wout_hbm, wout),
                (picked_hbm, picked_ref),
                (counts_hbm, counts_ref),
            )
        )
    ]
    for load in loads:
        load.start()

    loads[0].wait()
    wide[...] = proj[...].astype(F32)
    qkv_copies = []
    for j in range(local_heads):
        for s in range(n_seq):
            for c in range(3):
                first = c * heads + s * local_heads + j
                qkv_out[j, s, c] = wide[pl.ds(first, toks, stride=3 * heads), :].astype(BF)
        if j == 0:
            pl.semaphore_wait(barrier, greeted)
        sent = []
        for d in range(1, n_seq):
            peer = lax.rem(me_s + d, n_seq)
            copy = pltpu.make_async_remote_copy(
                src_ref=qkv_out.at[j, peer],
                dst_ref=qkv_in.at[j, :, me_s],
                send_sem=qkv_send.at[j, d],
                recv_sem=qkv_recv.at[j, d],
                device_id=(me_e, peer),
                device_id_type=MESH,
            )
            copy.start()
            sent.append(copy)
        own = pltpu.make_async_copy(qkv_out.at[j, me_s], qkv_in.at[j, :, me_s], qkv_own.at[j])
        own.start()
        qkv_copies.append((sent, own))

    for load in loads[6:]:
        load.wait()

    row_ids = lax.broadcasted_iota(jnp.int32, (slots, toks), 0)
    col_ids = lax.broadcasted_iota(jnp.int32, (toks, slots), 1)
    row_pos = jnp.full((slots, toks), -1, jnp.int32)
    col_pos = jnp.full((toks, slots), -1, jnp.int32)
    for e in range(n_exp):
        for c in range(cap):
            pos = jnp.where(c < counts_ref[0, e], picked_ref[c, e] - me_s * toks, -1)
            row_pos = jnp.where(row_ids == e * cap + c, pos, row_pos)
            col_pos = jnp.where(col_ids == e * cap + c, pos, col_pos)
    pick_rows = row_pos == lax.broadcasted_iota(jnp.int32, (slots, toks), 1)
    pick_cols = col_pos == lax.broadcasted_iota(jnp.int32, (toks, slots), 0)
    pick_rows = jnp.where(pick_rows, 1.0, 0.0).astype(BF)
    pick_cols = jnp.where(pick_cols, 1.0, 0.0)

    score_scale = 1.0 / math.sqrt(head)
    group = min(512 // toks, n_seq)
    att_copies = []

    def send_heads_to(j, d):
        peer = lax.rem(me_s + d, n_seq)
        copy = pltpu.make_async_remote_copy(
            src_ref=att_out.at[j, peer],
            dst_ref=att_in.at[j, me_s],
            send_sem=att_send.at[j, d],
            recv_sem=att_recv.at[j, d],
            device_id=(me_e, peer),
            device_id_type=MESH,
        )
        copy.start()
        return copy

    def keep_heads(j):
        own = pltpu.make_async_copy(att_out.at[j, me_s], att_in.at[j, me_s], att_own.at[j])
        own.start()
        return own

    def send_back_heads(j):
        sent = [send_heads_to(j, d) for d in range(1, n_seq)]
        att_copies.append((sent, keep_heads(j)))

    for j in range(local_heads):
        sent, own = qkv_copies[j]
        if 0 < j == local_heads - 1:
            for copy in sent:
                copy.wait_send()
            for earlier in range(j):
                send_back_heads(earlier)
        own.wait()
        for copy in sent:
            copy.wait_recv()

        last = j == local_heads - 1
        held = 1 if last else group

        def attend(b, carry, j=j, held=held):
            at = pl.ds(b * held, held)
            queries = qkv_in[j, 0, at].reshape(held * toks, head)
            keys = qkv_in[j, 1].reshape(length, head)
            values = qkv_in[j, 2].reshape(length, head)
            scores = lax.dot_general(
                queries, keys, (((1,), (1,)), ((), ())), preferred_element_type=F32
            )
            scores = scores * score_scale
            weights = jnp.exp(scores - jnp.max(scores, axis=-1, keepdims=True))
            weights = weights * (1.0 / jnp.sum(weights, axis=-1, keepdims=True))
            mixed = jnp.dot(weights.astype(BF), values, preferred_element_type=F32)
            att_out[j, at] = mixed.astype(BF).reshape(held, toks, head)
            return carry

        if last:
            sent = []
            for d in offsets:
                peer = lax.rem(me_s + d, n_seq)
                attend(peer, 0)
                if d:
                    sent.append(send_heads_to(j, d))
            att_copies.append((sent, keep_heads(j)))
        elif n_seq == group:
            attend(0, 0)
        else:
            lax.fori_loop(0, n_seq // group, attend, 0)

    for load in loads[1:6]:
        load.wait()
    for j in range(local_heads):
        sent, own = att_copies[j]
        own.wait()
        for copy in sent:
            copy.wait_recv()
        for s in range(n_seq):
            first = (s * local_heads + j) * head
            at = slice(first, first + head)
            resid[:, at] = hidden_in[:, at].astype(F32) + mod[0:1, at] * att_in[j, s].astype(F32)

    residual = resid[...]
    centred = residual - jnp.mean(residual, axis=-1, keepdims=True)
    variance = jnp.mean(centred * centred, axis=-1, keepdims=True)
    normed = centred * lax.rsqrt(variance + epsilon_norm)
    modulated = (normed * (1.0 + mod[2:3, :]) + mod[1:2, :]).astype(BF)

    parts = rows_in.shape[0]
    depth = pieces // parts

    def columns(part, k):
        return slice((part * depth + k) * head, (part * depth + k + 1) * head)

    def part_columns(part):
        return slice(part * depth * head, (part + 1) * depth * head)

    picked_rows = jnp.dot(pick_rows, modulated, preferred_element_type=F32)
    for part in range(parts):
        for k in range(depth):
            stage[pl.ds(k, slots, stride=depth), :] = picked_rows[:, columns(part, k)]
        rows_out[part] = stage[0 : slots * depth, :].reshape(rows_out.shape[1:]).astype(BF)

        def send_rows(peer_e, peer_s, part=part):
            pltpu.make_async_remote_copy(
                src_ref=rows_out.at[part, peer_e],
                dst_ref=rows_in.at[part, me],
                send_sem=row_send.at[part],
                recv_sem=row_recv.at[part],
                device_id=(peer_e, peer_s),
                device_id_type=MESH,
            ).start()

        to_all(send_rows)
        pltpu.make_async_copy(
            rows_out.at[part, me_e], rows_in.at[part, me], row_recv.at[part]
        ).start()

    gates = jax.nn.sigmoid(
        lax.dot_general(
            modulated, router[...], (((1,), (1,)), ((), ())), preferred_element_type=F32
        )
    )
    gate_cols = jnp.zeros((toks, slots), F32)
    for e in range(n_exp):
        gate_cols = jnp.where(col_ids // cap == e, gates[:, e : e + 1], gate_cols)
    gate_cols = gate_cols * pick_cols
    gate_high = gate_cols.astype(BF)
    gate_low = (gate_cols - gate_high.astype(F32)).astype(BF)

    block = rows_x.shape[0]
    sources = block // cap
    single = devices == sources

    def rows_arrive(part):
        pltpu.make_async_copy(rows_in.at[part], rows_in.at[part], row_recv.at[part]).wait()

    def send_part(part):
        def send_back(peer_e, peer_s):
            pltpu.make_async_remote_copy(
                src_ref=ret_out.at[part, peer_e * n_seq + peer_s],
                dst_ref=ret_in.at[part, me],
                send_sem=ret_send.at[part],
                recv_sem=ret_recv.at[part],
                device_id=(peer_e, peer_s),
                device_id_type=MESH,
            ).start()

        to_all(send_back)
        pltpu.make_async_copy(
            ret_out.at[part, me], ret_in.at[part, me], ret_recv.at[part]
        ).start()

    def apply_expert(b, carry):
        at = pl.ds(b * sources, sources)
        product = jnp.zeros((block, win.shape[1]), F32)
        for part in range(parts):
            if single:
                rows_arrive(part)
            stage[0 : block * depth, :] = (
                rows_in[part, at].astype(F32).reshape(block * depth, head)
            )
            for k in range(depth):
                rows_x[:, columns(part, k)] = stage[pl.ds(k, block, stride=depth), :].astype(BF)
            span = part_columns(part)
            product += jnp.dot(rows_x[:, span], win[span, :], preferred_element_type=F32)
        units = jax.nn.gelu(product, approximate=True).astype(BF)
        for part in range(parts):
            partial = jnp.dot(units, wout[:, part_columns(part)], preferred_element_type=F32)
            for k in range(depth):
                stage[pl.ds(k, block, stride=depth), :] = partial[:, k * head : (k + 1) * head]
            ret_out[part, at] = (
                stage[0 : block * depth, :].reshape(sources, cap * depth, head).astype(BF)
            )
            if single:
                send_part(part)
        return carry

    if single:
        apply_expert(0, 0)
    else:
        for part in range(parts):
            rows_arrive(part)
        lax.fori_loop(0, devices // sources, apply_expert, 0)
        for part in range(parts):
            send_part(part)

    for j in range(local_heads):
        if not 0 < j == local_heads - 1:
            for copy in qkv_copies[j][0]:
                copy.wait_send()
        for copy in att_copies[j][0]:
            copy.wait_send()
    for part in range(parts):
        others = rows_in.at[part, pl.ds(0, devices - 1)]
        pltpu.make_async_copy(others, others, row_send.at[part]).wait()

    for part in range(parts):
        pltpu.make_async_copy(ret_in.at[part], ret_in.at[part], ret_recv.at[part]).wait()
        for e in range(n_exp):
            summed = jnp.sum(ret_in[part, e * n_seq : (e + 1) * n_seq].astype(F32), axis=0)
            stage[e * cap * depth : (e + 1) * cap * depth, :] = summed
        for k in range(depth):
            rows_e[:, columns(part, k)] = stage[pl.ds(k, slots, stride=depth), :].astype(BF)
        span = part_columns(part)
        expert_rows = rows_e[:, span]
        mixture = jnp.dot(gate_high, expert_rows, preferred_element_type=F32) + jnp.dot(
            gate_low, expert_rows, preferred_element_type=F32
        )
        out_ref[:, span] = (resid[:, span] + mod[3:4, span] * mixture).astype(BF)

    for part in range(parts):
        others = ret_in.at[part, pl.ds(0, devices - 1)]
        pltpu.make_async_copy(others, others, ret_send.at[part]).wait()


def per_device(
    n_exp, n_seq, projected, hidden_in, modulation, w_router, picked, counts, weight_in, weight_out
):
    _, toks, three, heads, head = projected.shape
    width = hidden_in.shape[2]
    units = weight_in.shape[2]
    experts = w_router.shape[1]
    cap = picked.shape[3]
    devices = n_exp * n_seq
    slots = experts * cap
    pieces = width // head
    parts = 1
    depth = pieces // parts
    local_heads = heads // n_seq
    block = min(64, devices * cap)
    dma = pltpu.SemaphoreType.DMA
    anywhere = pl.BlockSpec(memory_space=pl.ANY)
    rows = toks * three * heads
    flops = (
        4 * local_heads * (toks * n_seq) ** 2 * head + 4 * devices * cap * width * units
    )
    out = pl.pallas_call(
        functools.partial(block_kernel, n_exp, n_seq, heads, cap),
        out_shape=jax.ShapeDtypeStruct((toks, width), BF),
        in_specs=[anywhere] * 8,
        out_specs=pl.BlockSpec(memory_space=pltpu.VMEM),
        scratch_shapes=[
            pltpu.SMEM((cap, experts), jnp.int32),
            pltpu.SMEM((1, experts), jnp.int32),
            pltpu.VMEM((rows, head), BF),
            pltpu.VMEM((toks, width), BF),
            pltpu.VMEM((4, width), F32),
            pltpu.VMEM((experts, width), BF),
            pltpu.VMEM((width, units), BF),
            pltpu.VMEM((units, width), BF),
            pltpu.VMEM((rows, head), F32),
            pltpu.VMEM((local_heads, n_seq, three, toks, head), BF),
            pltpu.VMEM((local_heads, three, n_seq, toks, head), BF),
            pltpu.VMEM((local_heads, n_seq, toks, head), BF),
            pltpu.VMEM((local_heads, n_seq, toks, head), BF),
            pltpu.VMEM((toks, width), F32),
            pltpu.VMEM((max(block, slots) * depth, head), F32),
            pltpu.VMEM((parts, experts, cap * depth, head), BF),
            pltpu.VMEM((parts, devices, cap * depth, head), BF),
            pltpu.VMEM((block, width), BF),
            pltpu.VMEM((parts, devices, cap * depth, head), BF),
            pltpu.VMEM((parts, devices, cap * depth, head), BF),
            pltpu.VMEM((slots, width), BF),
            dma((8,)),
            dma((local_heads, n_seq)),
            dma((local_heads, n_seq)),
            dma((local_heads,)),
            dma((local_heads, n_seq)),
            dma((local_heads, n_seq)),
            dma((local_heads,)),
            dma((parts,)),
            dma((parts,)),
            dma((parts,)),
            dma((parts,)),
        ],
        compiler_params=pltpu.CompilerParams(
            collective_id=0, has_side_effects=True, vmem_limit_bytes=56 * 1024 * 1024
        ),
        cost_estimate=pl.CostEstimate(
            flops=flops, bytes_accessed=4 * width * units, transcendentals=0
        ),
    )(
        picked.reshape(experts, cap).T,
        counts.reshape(1, experts),
        projected.reshape(rows, head),
        hidden_in[0],
        modulation[0],
        w_router.T,
        weight_in[0],
        weight_out[0],
    )
    return out[None]


def solution(mesh):
    in_specs = (
        P("exp", "seq", None, None, None),
        P("exp", "seq", None),
        P("exp", None, None),
        P(),
        P("exp", "seq", None, None),
        P("exp", "seq", None),
        P("exp", None, "seq"),
        P("exp", "seq", None),
    )
    out_specs = P("exp", "seq", None)
    return jax.shard_map(
        functools.partial(per_device, mesh.shape["exp"], mesh.shape["seq"]),
        mesh=mesh,
        in_specs=in_specs,
        out_specs=out_specs,
        check_vma=False,
    )
```
